256 devices in a mesh: tensor: 8 (over z_lo, y), grow: 4 (over x), gcol: 8 (over z_hi, core).
Axes of the slice: x: 4, y: 4, z: 8 (z_hi: 4, z_lo: 2; z = z_hi * 2 + z_lo), core: 2. Of those that a mesh axis runs over, the one named last changes fastest.
Arguments:
- hidden: bfloat16 [2048, 8192], P(None, 'grow'), may hold values from -6 to 6
- gain: float32 [8192], P('grow'), may hold values from 0.5 to 2
- gate_weight: bfloat16 [8192, 14336], P('grow', ('tensor', 'gcol')), may hold values from -0.0625 to 0.0625
- up_weight: bfloat16 [8192, 14336], P('grow', ('tensor', 'gcol')), may hold values from -0.0625 to 0.0625
Outputs:
- moments: float32 [14336, 8, 1792], P(('tensor', 'grow'), 'gcol')
The draws below stay inside these ranges and needn't reach their ends.
All inputs are finite; a program needn't handle non-finite values.
Results may differ from the reference program's by a relative error of at most 0.0065.
Values may be sent and summed in bfloat16 or wider, within the bound.
No kernel may reach another device: no remote copies, remote signals or barrier semaphores. Data moves between devices by JAX's collectives and lax.ppermute only.
A program may use at most 128 MiB of HBM per device.

```python
import math
import jax
import jax.numpy as jnp
from jax import lax

D = 8192
FFW = 14336
TOKENS = 2048
N_TENSOR = 8
N_GCOL = 8


def block_scale(rng, dims, pieces, low, high):
    loudness, own = 1.0, jax.random.fold_in(rng, 6)
    for position, shards_of in pieces:
        steps = jnp.exp(jax.random.uniform(jax.random.fold_in(own, position), (shards_of,), jnp.float32, low / len(pieces), high / len(pieces)))
        loudness = loudness * jnp.repeat(steps, dims[position] // shards_of).reshape([-1 if axis == position else 1 for axis in range(len(dims))])
    return loudness


def normal_values(stream_key, dims, scale, bound, cuts=(), held_as=jnp.bfloat16):
    drawn = jax.random.normal(stream_key, dims, jnp.float32) * scale
    if len(cuts) > 0:
        drawn = block_scale(stream_key, dims, cuts, -0.22, 0.18) * drawn
    return jnp.clip(drawn, min=-bound, max=bound).astype(held_as)


def setup_inputs(seed: int = 0) -> dict:
    key_of = jax.random.split(jax.random.key(seed), 5)
    return {
        "hidden": normal_values(key_of[0], (TOKENS, D), 1.0, 6.0, ((1, 4),)),
        "gain": jnp.clip(jnp.exp(math.log(2.0) - 1.3862944 * jax.random.uniform(key_of[1], (D,), jnp.float32) ** block_scale(key_of[1], (D,), ((0, 4),), -0.2, 0.2)), 0.5, 2.0),
        "gate_weight": normal_values(key_of[2], (D, FFW), D ** -0.5, 0.0625, ((0, 4), (1, 64))),
        "up_weight": normal_values(key_of[3], (D, FFW), D ** -0.5, 0.0625, ((0, 4), (1, 64))),
    }


EPS = 1e-05

def reference(hidden, gain, gate_weight, up_weight):
    values = hidden.astype(jnp.float32)
    total = lax.optimization_barrier(jnp.sum(values * values, axis=1, keepdims=True))
    scale = lax.rsqrt(total / D + EPS)
    normed = (values * gain[None, :] * scale).astype(jnp.bfloat16)
    gate = jnp.dot(normed, gate_weight, preferred_element_type=jnp.float32)
    up = jnp.dot(normed, up_weight, preferred_element_type=jnp.float32)
    keys = (jax.nn.silu(gate) * up).astype(jnp.bfloat16)
    second = lax.dot_general(keys, keys, (((0,), (0,)), ((), ())), preferred_element_type=jnp.float32)
    second = second / TOKENS
    block = FFW // (N_TENSOR * N_GCOL)
    second = second.reshape(FFW, N_TENSOR, N_GCOL, block)
    second = jnp.transpose(second, (0, 2, 1, 3))
    return second.reshape(FFW, N_GCOL, N_TENSOR * block)
```

```python
import jax
import jax.numpy as jnp
from jax import lax
from jax.experimental import pallas as pl
from jax.experimental.pallas import tpu as pltpu
from jax.sharding import Mesh, PartitionSpec as P

D = 8192
EPS = 1e-05
TINY = 1e-30
F32 = jnp.float32
BF16 = jnp.bfloat16
NT = (((1,), (1,)), ((), ()))
VMEM_LIMIT = 48 * 1024 * 1024
PAD = 16


def shift(value, axis, n, by):
    return lax.ppermute(value, axis, [(i, (i + by) % n) for i in range(n)])


def encode(v):
    s = v * v
    s = s * s
    return jnp.where(v < 0, -s, s).astype(BF16)


def decode(y):
    y = y.astype(F32)
    m = jnp.sqrt(jnp.sqrt(jnp.abs(y)))
    return jnp.where(y < 0, -m, m)


def sumsq_row(h):
    v = h.astype(F32)
    v = v * v
    lanes = v[:, 0:128]
    for i in range(1, v.shape[1] // 128):
        lanes = lanes + v[:, i * 128 : (i + 1) * 128]
    return jnp.sum(lanes.T, axis=0, keepdims=True)


def emit_send(part, squares, o_ref):
    rows = part.shape[0]
    r = lax.rsqrt(squares + TINY)
    o_ref[0:rows, :] = encode(part * r)
    hi = squares.astype(BF16).astype(F32)
    rest = squares - hi
    mid = rest.astype(BF16).astype(F32)
    lo = rest - mid
    at = lax.broadcasted_iota(jnp.int32, (PAD, squares.shape[1]), 0)
    tile = jnp.where(at == 0, hi, jnp.where(at == 1, mid, jnp.where(at == 2, lo, 0.0)))
    o_ref[rows : rows + PAD, :] = tile.astype(BF16)


def first_kernel(idx_ref, gw_ref, uw_ref, gain_ref, h_ref, w_ref, o_ref):
    width = gw_ref.shape[0]

    @pl.when(pl.program_id(0) == 0)
    def _():
        g = gain_ref[...]
        w_ref[0:width, :] = (gw_ref[...].astype(F32) * g).astype(BF16)
        w_ref[width : 2 * width, :] = (uw_ref[...].astype(F32) * g).astype(BF16)

    part = lax.dot_general(w_ref[...], h_ref[...], NT, preferred_element_type=F32)
    emit_send(part, sumsq_row(h_ref[...]), o_ref)


def send_kernel(idx_ref, w_ref, h_ref, o_ref):
    part = lax.dot_general(w_ref[...], h_ref[...], NT, preferred_element_type=F32)
    emit_send(part, sumsq_row(h_ref[...]), o_ref)


def own_kernel(idx_ref, w_ref, h_ref, o_ref):
    rows = w_ref.shape[0]
    part = lax.dot_general(w_ref[...], h_ref[...], NT, preferred_element_type=F32)
    o_ref[0:rows, :] = part
    o_ref[rows : rows + 8, :] = jnp.broadcast_to(sumsq_row(h_ref[...]), (8, part.shape[1]))


def keys_kernel(own_ref, p_ref, q_ref, r_ref, a_ref, b_ref):
    rows = own_ref.shape[0] - 8
    width = rows // 2
    total = own_ref[rows : rows + 1, :]
    norms = []
    for ref in (p_ref, q_ref, r_ref):
        s = ref[rows : rows + PAD, :].astype(F32)
        s = s[0:1, :] + (s[1:2, :] + s[2:3, :])
        norms.append(jnp.sqrt(s + TINY))
        total = total + s
    scale = lax.rsqrt(total / D + EPS)
    mixed = own_ref[0:rows, :]
    for ref, norm in zip((p_ref, q_ref, r_ref), norms):
        mixed = mixed + decode(ref[0:rows, :]) * norm
    mixed = mixed * scale
    gate, up = mixed[0:width, :], mixed[width:rows, :]
    keys = (gate / (1.0 + jnp.exp(-gate)) * up).astype(BF16)
    half = keys.shape[1] // 2
    a_ref[...] = keys[:, 0:half]
    b_ref[...] = keys[:, half:]


def block_call(kernel, idx, h, ins, in_specs, out_shape, out_specs, flops, tile):
    per = 512 // tile
    return pl.pallas_call(
        kernel,
        grid_spec=pltpu.PrefetchScalarGridSpec(
            num_scalar_prefetch=1,
            grid=(per,),
            in_specs=in_specs + [pl.BlockSpec((tile, h.shape[1]), lambda i, s: (s[0] * per + i, 0))],
            out_specs=out_specs,
        ),
        out_shape=out_shape,
        compiler_params=pltpu.CompilerParams(vmem_limit_bytes=VMEM_LIMIT),
        cost_estimate=pl.CostEstimate(flops=flops, bytes_accessed=h.shape[1] * 512 * 2, transcendentals=0),
    )(idx, *ins, h)


def moment_kernel(idx_ref, *refs):
    n_col, n_row = 64, 16
    cols, rows = refs[:n_col], refs[n_col : n_col + n_row]
    o_ref, c_buf, r_buf, sem = refs[n_col + n_row :]
    zl, y, x, zh, c = (idx_ref[i] for i in range(5))
    n_tok = 256

    @pl.when(pl.program_id(0) == 0)
    def _():
        copies = []
        k = 0
        for half in range(2):
            for dz in range(2):
                for dy in range(4):
                    for dx in range(4):
                        t = lax.rem(zl + dz, 2) * 4 + lax.rem(y + dy, 4)
                        s = lax.rem(x + dx, 4) * 2 + half
                        copies.append(pltpu.make_async_copy(cols[k], c_buf.at[s, t], sem.at[0]))
                        k += 1
        k = 0
        for half in range(2):
            for d in range(4):
                for dc in range(2):
                    s = lax.rem(zh + d, 4) * 2 + half
                    copies.append(pltpu.make_async_copy(rows[k], r_buf.at[s, lax.rem(c + dc, 2)], sem.at[0]))
                    k += 1
        for cp in copies:
            cp.start()
        for cp in copies:
            cp.wait()

    n = pl.program_id(0)
    at = pl.multiple_of(n * 256, 256)
    n_rows = 2 * r_buf.shape[2]
    acc = None
    for s in range(8):
        left = r_buf[s].reshape(n_rows, n_tok)
        right = c_buf.reshape(8, 8 * 224, n_tok)[s, pl.ds(at, 256), :]
        d = lax.dot_general(left, right, NT, preferred_element_type=F32)
        acc = d if acc is None else acc + d
    o_ref[:, 0, :] = acc * (1.0 / 2048)


def gather4(v, axis):
    up = shift(v, axis, 4, -1)
    down = shift(v, axis, 4, 1)
    return up, down


def shards(hidden, gain, gate_weight, up_weight):
    zl, y, x, zh, c = (lax.axis_index(a) for a in ("zl", "y", "x", "zh", "c"))
    features = hidden.shape[1]
    width = gate_weight.shape[1]
    rows = 2 * width
    gw, uw = gate_weight.T, up_weight.T
    g2 = gain[None, :]
    flops = 2 * 512 * features * rows
    tile = 256

    def idx(d):
        return lax.rem(x + d, 4).astype(jnp.int32)[None]

    whole = lambda shape: pl.BlockSpec(shape, lambda i, s: (0, 0))
    send_shape = jax.ShapeDtypeStruct((rows + PAD, 512), BF16)
    send_spec = pl.BlockSpec((rows + PAD, tile), lambda i, s: (0, i))
    w, block2 = block_call(
        first_kernel, idx(2), hidden, (gw, uw, g2),
        [whole((width, features)), whole((width, features)), whole((1, features))],
        (jax.ShapeDtypeStruct((rows, features), BF16), send_shape),
        (whole((rows, features)), send_spec), flops, tile,
    )
    got2 = shift(block2, "x", 4, 2)
    block1 = block_call(send_kernel, idx(1), hidden, (w,), [whole((rows, features))], send_shape, send_spec, flops, tile)
    got1 = shift(block1, "x", 4, 1)
    block3 = block_call(send_kernel, idx(3), hidden, (w,), [whole((rows, features))], send_shape, send_spec, flops, tile)
    got3 = shift(block3, "x", 4, -1)
    own = block_call(
        own_kernel, idx(0), hidden, (w,), [whole((rows, features))],
        jax.ShapeDtypeStruct((rows + 8, 512), F32), pl.BlockSpec((rows + 8, tile), lambda i, s: (0, i)), flops, tile,
    )
    half_shape = jax.ShapeDtypeStruct((width, 256), BF16)
    keys = pl.pallas_call(
        keys_kernel,
        out_shape=(half_shape, half_shape),
        compiler_params=pltpu.CompilerParams(vmem_limit_bytes=VMEM_LIMIT),
    )(own, got1, got2, got3)

    def ring(v, axis, way):
        up = shift(v, axis, 4, -1)
        down = shift(v, axis, 4, 1)
        far = shift(up, axis, 4, -1) if way else shift(down, axis, 4, 1)
        return [v, up, far, down]

    columns = []
    for half, order in ((0, ("y", "x")), (1, ("x", "y"))):
        mine = keys[half]
        pair = [mine, shift(mine, "zl", 2, 1)]
        table = {}
        for dz in range(2):
            for i, v in enumerate(ring(pair[dz], order[0], dz)):
                for j, u in enumerate(ring(v, order[1], (dz + i) % 2)):
                    dy, dx = (i, j) if order[0] == "y" else (j, i)
                    table[dz, dy, dx] = u
        columns += [table[dz, dy, dx] for dz in range(2) for dy in range(4) for dx in range(4)]

    flip = [(i * 4 + j, j * 4 + i) for i in range(4) for j in range(4)]
    row_list = []
    for half in range(2):
        moved = lax.ppermute(keys[half], ("x", "zh"), flip)
        for v in ring(moved, "zh", half):
            row_list += [v, shift(v, "c", 2, 1)]

    place = jnp.stack([zl, y, x, zh, c]).astype(jnp.int32)
    any_spec = pl.BlockSpec(memory_space=pl.ANY)
    return pl.pallas_call(
        moment_kernel,
        grid_spec=pltpu.PrefetchScalarGridSpec(
            num_scalar_prefetch=1,
            grid=(7,),
            in_specs=[any_spec] * (64 + 16),
            out_specs=pl.BlockSpec((rows, 1, 256), lambda i, s: (0, 0, i)),
            scratch_shapes=[
                pltpu.VMEM((8, 8, width, 256), BF16),
                pltpu.VMEM((8, 2, width, 256), BF16),
                pltpu.SemaphoreType.DMA((1,)),
            ],
        ),
        out_shape=jax.ShapeDtypeStruct((rows, 1, 8 * width), F32),
        compiler_params=pltpu.CompilerParams(vmem_limit_bytes=VMEM_LIMIT),
    )(place, *columns, *row_list)


def solution(mesh):
    fine = Mesh(mesh.devices.reshape(2, 4, 4, 4, 2), ("zl", "y", "x", "zh", "c"))
    cols = ("zl", "y", "zh", "c")
    in_specs = (P(None, "x"), P("x"), P("x", cols), P("x", cols))
    out_specs = P(("zl", "y", "x"), ("zh", "c"), None)
    return jax.shard_map(shards, mesh=fine, in_specs=in_specs, out_specs=out_specs, check_vma=False)
```

```python
import jax
import jax.numpy as jnp
from jax import lax
from jax.experimental import pallas as pl
from jax.experimental.pallas import tpu as pltpu
from jax.sharding import Mesh, PartitionSpec as P

D = 8192
EPS = 1e-05
TINY = 1e-30
F32 = jnp.float32
BF16 = jnp.bfloat16
NT = (((1,), (1,)), ((), ()))
PAD = 16


def shift(value, axis, n, by):
    return lax.ppermute(value, axis, [(i, (i + by) % n) for i in range(n)])


def encode(v):
    s = v * v
    s = s * s
    return jnp.where(v < 0, -s, s).astype(BF16)


def decode(y):
    y = y.astype(F32)
    q = lax.rsqrt(jnp.maximum(jnp.abs(y), TINY))
    return (y * q) * (q * lax.rsqrt(q))


def sumsq_row(h):
    v = h.astype(F32)
    v = v * v
    lanes = v[:, 0:128]
    for i in range(1, v.shape[1] // 128):
        lanes = lanes + v[:, i * 128 : (i + 1) * 128]
    return jnp.sum(lanes.T, axis=0, keepdims=True)


def emit_send(part, squares, o_ref, at_token):
    rows = part.shape[0]
    r = lax.rsqrt(squares + TINY)
    tokens = slice(at_token, at_token + part.shape[1])
    o_ref[0:rows, tokens] = encode(part * r)
    hi = squares.astype(BF16).astype(F32)
    rest = squares - hi
    mid = rest.astype(BF16).astype(F32)
    lo = rest - mid
    at = lax.broadcasted_iota(jnp.int32, (PAD, squares.shape[1]), 0)
    tile = jnp.where(at == 0, hi, jnp.where(at == 1, mid, jnp.where(at == 2, lo, 0.0)))
    o_ref[rows : rows + PAD, tokens] = tile.astype(BF16)


def first_kernel(idx_ref, gain_ref, gw_ref, uw_ref, h_ref, w_ref, o_ref, gu_buf, h_buf, sem):
    width = gw_ref.shape[0]
    at = pl.ds(pl.multiple_of(idx_ref[0] * 512, 512), 512)
    loads = [
        pltpu.make_async_copy(gw_ref, gu_buf.at[0], sem.at[0]),
        pltpu.make_async_copy(uw_ref, gu_buf.at[1], sem.at[1]),
        pltpu.make_async_copy(h_ref.at[at, :], h_buf, sem.at[2]),
    ]
    for cp in loads:
        cp.start()
    loads[0].wait()
    loads[1].wait()
    g = gain_ref[...]
    for i in range(2):
        w_ref[i * width : (i + 1) * width, :] = (gu_buf[i].astype(F32) * g).astype(BF16)
    loads[2].wait()
    part = lax.dot_general(w_ref[...], h_buf[...], NT, preferred_element_type=F32)
    emit_send(part, sumsq_row(h_buf[...]), o_ref, 0)


def fetch(idx_ref, h_ref, h_buf, sem):
    copies = []
    for j in range(h_buf.shape[0]):
        at = pl.ds(pl.multiple_of(idx_ref[j] * 512, 512), 512)
        copies.append(pltpu.make_async_copy(h_ref.at[at, :], h_buf.at[j], sem.at[j]))
    for cp in copies:
        cp.start()
    for cp in copies:
        cp.wait()


def send_kernel(idx_ref, w_ref, h_ref, o_ref, p_ref, h_buf, sem):
    fetch(idx_ref, h_ref, h_buf, sem)
    for k, ref in enumerate((o_ref, p_ref)):
        part = lax.dot_general(w_ref[...], h_buf[k], NT, preferred_element_type=F32)
        emit_send(part, sumsq_row(h_buf[k]), ref, 0)


def own_kernel(idx_ref, w_ref, h_ref, o_ref, h_buf, sem):
    rows = w_ref.shape[0]
    fetch(idx_ref, h_ref, h_buf, sem)
    o_ref[0:rows, :] = lax.dot_general(w_ref[...], h_buf[0], NT, preferred_element_type=F32)
    o_ref[rows : rows + 8, :] = jnp.broadcast_to(sumsq_row(h_buf[0]), (8, o_ref.shape[1]))


def keys_kernel(own_ref, p_ref, q_ref, r_ref, k_ref):
    rows = own_ref.shape[0] - 8
    width = rows // 2
    total = own_ref[rows : rows + 1, :]
    norms = []
    for ref in (p_ref, q_ref, r_ref):
        s = ref[rows : rows + PAD, :].astype(F32)
        s = s[0:1, :] + (s[1:2, :] + s[2:3, :])
        norms.append(jnp.sqrt(s + TINY))
        total = total + s
    scale = lax.rsqrt(total / D + EPS)
    mixed = own_ref[0:rows, :]
    for ref, norm in zip((p_ref, q_ref, r_ref), norms):
        mixed = mixed + decode(ref[0:rows, :]) * norm
    mixed = mixed * scale
    gate, up = mixed[0:width, :], mixed[width:rows, :]
    k_ref[...] = (gate / (1.0 + jnp.exp(-gate)) * up).astype(BF16)


ORDER = (0, 1, 3, 2)
WIDTH_TILE = 256


def lanes(s, tokens):
    return pl.ds(pl.multiple_of(lax.rem(s, 4) * tokens, tokens), tokens)


def places(t, width):
    return pl.ds(pl.multiple_of(t * width, width), width)


def put_own(cols, ref, idx_ref, d, ks):
    width = cols.shape[0] // 8
    zl, y, x = idx_ref[0], idx_ref[1], idx_ref[2]
    for i, k in enumerate(ks):
        at = places(zl * 4 + lax.rem(y + ORDER[k], 4), width)
        cols[at, lanes(x + d, 512)] = ref[i * width : (i + 1) * width, :]


def put_far(cols, ref, idx_ref, d, ks):
    width = cols.shape[0] // 8
    zl, y, x = idx_ref[0], idx_ref[1], idx_ref[2]
    for i, k in enumerate(ks):
        at = places((1 - zl) * 4 + lax.rem(y + d, 4), width)
        cols[at, lanes(x + ORDER[k], 512)] = ref[i * width : (i + 1) * width, :]


def own_cols_kernel(idx_ref, own_ref, up_ref, down_ref, cols, a_ref, b_ref):
    half = a_ref.shape[0]
    a_ref[...] = down_ref[0:half, :]
    b_ref[...] = up_ref[half:, :]
    for d, ref in ((0, own_ref), (1, up_ref), (3, down_ref)):
        put_own(cols, ref, idx_ref, d, range(4))


def far_kernel(idx_ref, cols_in, far_ref, up_ref, down_ref, cols, a_ref, b_ref):
    half = a_ref.shape[0]
    a_ref[...] = down_ref[0:half, :]
    b_ref[...] = up_ref[half:, :]
    for d, ref in ((0, far_ref), (1, up_ref), (3, down_ref)):
        put_far(cols, ref, idx_ref, d, range(4))


def moment_kernel(idx_ref, cols_in, own_a, own_b, far_a, far_b, r0, r1, s0, s1, o_ref, cols, r_buf, o_buf, sem):
    width = cols.shape[0] // 8
    zh, c = idx_ref[3], idx_ref[4]
    for n, pair in enumerate(((r0, r1), (s0, s1))):
        core = lax.rem(c + n, 2)
        for j, ref in enumerate(pair):
            at = lanes(zh + 8 - j - 2 * core, 512)
            r_buf[places(core, width), at] = ref[0:width, :]
            r_buf[places(1 - core, width), at] = ref[width:, :]
    put_own(cols, own_a, idx_ref, 2, (0, 1))
    put_own(cols, own_b, idx_ref, 2, (2, 3))
    put_far(cols, far_a, idx_ref, 2, (0, 1))
    put_far(cols, far_b, idx_ref, 2, (2, 3))
    for n in range(cols.shape[0] // WIDTH_TILE):
        at = slice(n * WIDTH_TILE, (n + 1) * WIDTH_TILE)
        acc = lax.dot_general(r_buf[...], cols[at, :], NT, preferred_element_type=F32)
        o_buf[:, 0, at] = acc * (1.0 / 2048)
    cp = pltpu.make_async_copy(o_buf, o_ref, sem.at[0])
    cp.start()
    cp.wait()


SMEM = pl.BlockSpec(memory_space=pltpu.SMEM)
VMEM = pl.BlockSpec(memory_space=pltpu.VMEM)
HBM = pl.BlockSpec(memory_space=pltpu.HBM)
MIB = 1024 * 1024


def shards(hidden, gain, gate_weight, up_weight):
    zl, y, x, zh, c = (lax.axis_index(a).astype(jnp.int32) for a in ("zl", "y", "x", "zh", "c"))
    features = hidden.shape[1]
    width = gate_weight.shape[1]
    rows = 2 * width
    gw, uw = gate_weight.T, up_weight.T
    g2 = gain[None, :]
    flops = 2 * 512 * features * rows
    def call(kernel, in_specs, out_shape, out_specs, scratch, limit, cost, *ins):
        return pl.pallas_call(
            kernel,
            in_specs=in_specs,
            out_specs=out_specs,
            out_shape=out_shape,
            scratch_shapes=scratch,
            compiler_params=pltpu.CompilerParams(vmem_limit_bytes=limit),
            cost_estimate=pl.CostEstimate(flops=cost, bytes_accessed=2 * MIB, transcendentals=0),
        )(*ins)

    def at(*ds):
        return jnp.stack([lax.rem(x + d, 4) for d in ds])

    send_shape = jax.ShapeDtypeStruct((rows + PAD, 512), BF16)

    def h_scratch(n):
        return [pltpu.VMEM((n, 512, features), BF16), pltpu.SemaphoreType.DMA((n,))]

    w, block2 = call(
        first_kernel, [SMEM, VMEM, HBM, HBM, HBM],
        (jax.ShapeDtypeStruct((rows, features), BF16), send_shape), (VMEM, VMEM),
        [pltpu.VMEM((2, width, features), BF16), pltpu.VMEM((512, features), BF16), pltpu.SemaphoreType.DMA((3,))],
        57 * MIB, flops, at(2), g2, gw, uw, hidden,
    )
    got2 = shift(block2, "x", 4, 2)
    block1, block3 = call(
        send_kernel, [SMEM, VMEM, HBM], (send_shape, send_shape), (VMEM, VMEM),
        h_scratch(2), 53 * MIB, 2 * flops, at(1, 3), w, hidden,
    )
    got1 = shift(block1, "x", 4, 1)
    got3 = shift(block3, "x", 4, -1)
    own_part = call(
        own_kernel, [SMEM, VMEM, HBM], jax.ShapeDtypeStruct((rows + 8, 512), F32), VMEM,
        h_scratch(1), 53 * MIB, flops, at(0), w, hidden,
    )
    keys = call(
        keys_kernel, [VMEM] * 4, jax.ShapeDtypeStruct((width, 512), BF16), VMEM, [], 16 * MIB, flops, own_part, got1, got2, got3
    )

    def after(v, *others):
        return lax.optimization_barrier((v,) + others)[0]

    def join(*parts):
        return jnp.concatenate(parts, axis=0)

    def rows_to(j):
        return [
            ((i * 4 + k) * 2 + e, (k * 4 + (i + j + 2 * e) % 4) * 2 + e)
            for i in range(4) for k in range(4) for e in range(2)
        ]

    place = jnp.stack([zl, y, x, zh, c])
    columns = jax.ShapeDtypeStruct((8 * width, 2048), BF16)
    two = jax.ShapeDtypeStruct((rows, 512), BF16)

    partner = shift(keys, "zl", 2, 1)
    y1, y3 = shift(keys, "y", 4, -1), shift(keys, "y", 4, 1)
    both = join(keys, shift(keys, "c", 2, 1))
    r0 = lax.ppermute(both, ("x", "zh", "c"), rows_to(0))
    r1 = lax.ppermute(both, ("x", "zh", "c"), rows_to(1))
    x1, x3 = shift(partner, "x", 4, -1), shift(partner, "x", 4, 1)
    y2 = shift(after(keys, y1, y3), "y", 4, 2)
    x2 = shift(after(partner, x1, x3), "x", 4, 2)
    own = after(join(keys, y1, y3, y2), r0)
    own_x1, own_x3 = shift(own, "x", 4, -1), shift(own, "x", 4, 1)
    far = after(join(partner, x1, x3, x2), r1)
    far_y1, far_y3 = shift(far, "y", 4, -1), shift(far, "y", 4, 1)
    s0, s1 = shift(r0, "c", 2, 1), shift(r1, "c", 2, 1)
    cols, own_up, own_down = call(
        own_cols_kernel, [SMEM] + [VMEM] * 3, (columns, two, two), (VMEM,) * 3, [], 4 * MIB, flops // 4, place, own, own_x1, own_x3
    )
    own_x2a, own_x2b = shift(own_up, "x", 4, 1), shift(own_down, "x", 4, -1)
    cols, far_up, far_down = pl.pallas_call(
        far_kernel,
        in_specs=[SMEM] + [VMEM] * 4,
        out_specs=(VMEM,) * 3,
        out_shape=(columns, two, two),
        input_output_aliases={1: 0},
        compiler_params=pltpu.CompilerParams(vmem_limit_bytes=4 * MIB),
        cost_estimate=pl.CostEstimate(flops=flops // 4, bytes_accessed=2 * MIB, transcendentals=0),
    )(place, cols, far, far_y1, far_y3)
    far_y2a, far_y2b = shift(far_up, "y", 4, 1), shift(far_down, "y", 4, -1)
    return pl.pallas_call(
        moment_kernel,
        in_specs=[SMEM] + [VMEM] * 9,
        out_specs=(HBM, VMEM),
        out_shape=(jax.ShapeDtypeStruct((rows, 1, 8 * width), F32), columns),
        scratch_shapes=[
            pltpu.VMEM((rows, 2048), BF16),
            pltpu.VMEM((rows, 1, 8 * width), F32),
            pltpu.SemaphoreType.DMA((1,)),
        ],
        input_output_aliases={1: 1},
        compiler_params=pltpu.CompilerParams(vmem_limit_bytes=16 * MIB),
        cost_estimate=pl.CostEstimate(flops=4 * flops, bytes_accessed=4 * MIB, transcendentals=0),
    )(place, cols, own_x2a, own_x2b, far_y2a, far_y2b, r0, r1, s0, s1)[0]


def solution(mesh):
    fine = Mesh(mesh.devices.reshape(2, 4, 4, 4, 2), ("zl", "y", "x", "zh", "c"))
    cols = ("zl", "y", "zh", "c")
    in_specs = (P(None, "x"), P("x"), P("x", cols), P("x", cols))
    out_specs = P(("zl", "y", "x"), ("zh", "c"), None)
    return jax.shard_map(shards, mesh=fine, in_specs=in_specs, out_specs=out_specs, check_vma=False)
```

```python
import jax
import jax.numpy as jnp
from jax import lax
from jax.experimental import pallas as pl
from jax.experimental.pallas import tpu as pltpu
from jax.sharding import Mesh, PartitionSpec as P

D = 8192
EPS = 1e-05
TINY = 1e-30
F32 = jnp.float32
BF16 = jnp.bfloat16
NT = (((1,), (1,)), ((), ()))
PAD = 16


def shift(value, axis, n, by):
    return lax.ppermute(value, axis, [(i, (i + by) % n) for i in range(n)])


def encode(v):
    s = v * v
    s = s * s
    return jnp.where(v < 0, -s, s).astype(BF16)


def decode(y):
    y = y.astype(F32)
    q = lax.rsqrt(jnp.maximum(jnp.abs(y), TINY))
    return (y * q) * (q * lax.rsqrt(q))


def sumsq_row(h):
    v = h.astype(F32)
    v = v * v
    lanes = v[:, 0:128]
    for i in range(1, v.shape[1] // 128):
        lanes = lanes + v[:, i * 128 : (i + 1) * 128]
    return jnp.sum(lanes.T, axis=0, keepdims=True)


def emit_send(part, squares, o_ref, at_token):
    rows = part.shape[0]
    r = lax.rsqrt(squares + TINY)
    tokens = slice(at_token, at_token + part.shape[1])
    o_ref[0:rows, tokens] = encode(part * r)
    hi = squares.astype(BF16).astype(F32)
    rest = squares - hi
    mid = rest.astype(BF16).astype(F32)
    lo = rest - mid
    at = lax.broadcasted_iota(jnp.int32, (PAD, squares.shape[1]), 0)
    tile = jnp.where(at == 0, hi, jnp.where(at == 1, mid, jnp.where(at == 2, lo, 0.0)))
    o_ref[rows : rows + PAD, tokens] = tile.astype(BF16)


def first_kernel(idx_ref, gain_ref, gw_ref, uw_ref, h_ref, w_ref, o_ref, gu_buf, h_buf, sem):
    width = gw_ref.shape[0]
    at = pl.ds(pl.multiple_of(idx_ref[0] * 512, 512), 512)
    loads = [
        pltpu.make_async_copy(gw_ref, gu_buf.at[0], sem.at[0]),
        pltpu.make_async_copy(uw_ref, gu_buf.at[1], sem.at[1]),
        pltpu.make_async_copy(h_ref.at[at, :], h_buf, sem.at[2]),
    ]
    for cp in loads:
        cp.start()
    loads[0].wait()
    loads[1].wait()
    g = gain_ref[...]
    for i in range(2):
        w_ref[i * width : (i + 1) * width, :] = (gu_buf[i].astype(F32) * g).astype(BF16)
    loads[2].wait()
    part = lax.dot_general(w_ref[...], h_buf[...], NT, preferred_element_type=F32)
    emit_send(part, sumsq_row(h_buf[...]), o_ref, 0)


def fetch(idx_ref, h_ref, h_buf, sem):
    copies = []
    for j in range(h_buf.shape[0]):
        at = pl.ds(pl.multiple_of(idx_ref[j] * 512, 512), 512)
        copies.append(pltpu.make_async_copy(h_ref.at[at, :], h_buf.at[j], sem.at[j]))
    for cp in copies:
        cp.start()
    for cp in copies:
        cp.wait()


def send_kernel(idx_ref, w_ref, h_ref, o_ref, p_ref, h_buf, sem):
    fetch(idx_ref, h_ref, h_buf, sem)
    for k, ref in enumerate((o_ref, p_ref)):
        part = lax.dot_general(w_ref[...], h_buf[k], NT, preferred_element_type=F32)
        emit_send(part, sumsq_row(h_buf[k]), ref, 0)


def own_kernel(idx_ref, w_ref, h_ref, o_ref, h_buf, sem):
    rows = w_ref.shape[0]
    fetch(idx_ref, h_ref, h_buf, sem)
    o_ref[0:rows, :] = lax.dot_general(w_ref[...], h_buf[0], NT, preferred_element_type=F32)
    o_ref[rows : rows + 8, :] = jnp.broadcast_to(sumsq_row(h_buf[0]), (8, o_ref.shape[1]))


def keys_kernel(own_ref, p_ref, q_ref, r_ref, k_ref):
    rows = own_ref.shape[0] - 8
    width = rows // 2
    total = own_ref[rows : rows + 1, :]
    norms = []
    for ref in (p_ref, q_ref, r_ref):
        s = ref[rows : rows + PAD, :].astype(F32)
        s = s[0:1, :] + (s[1:2, :] + s[2:3, :])
        norms.append(jnp.sqrt(s + TINY))
        total = total + s
    scale = lax.rsqrt(total / D + EPS)
    mixed = own_ref[0:rows, :]
    for ref, norm in zip((p_ref, q_ref, r_ref), norms):
        mixed = mixed + decode(ref[0:rows, :]) * norm
    mixed = mixed * scale
    gate, up = mixed[0:width, :], mixed[width:rows, :]
    k_ref[...] = (gate / (1.0 + jnp.exp(-gate)) * up).astype(BF16)


ORDER = (0, 1, 3, 2)


def lanes(s, tokens):
    return pl.ds(pl.multiple_of(lax.rem(s, 4) * tokens, tokens), tokens)


def places(t, width):
    return pl.ds(pl.multiple_of(t * width, width), width)


def put(cols, ref, idx_ref, role, d, offsets, which, step=2):
    width = cols.shape[0] // 4
    y, x = idx_ref[1], idx_ref[2]
    for i, off in enumerate(offsets):
        row, lane = y + off + role * (d - off), x + d + role * (off - d)
        at = (step * i + which) * width
        cols[places(lax.rem(row, 4), width), lanes(lane, 512)] = ref[at : at + width, :]


def base_kernel(idx_ref, k_ref, k_other, p_ref, p_other, b_ref):
    width = k_ref.shape[0]
    for core, (first, second) in enumerate(((k_ref, k_other), (p_ref, p_other))):

        @pl.when(idx_ref[4] == core)
        def _():
            b_ref[0:width, :] = first[...]
            b_ref[width:, :] = second[...]


def pack_kernel(*refs):
    size = refs[0].shape[0]
    for i, ref in enumerate(refs[:4]):
        refs[4][i * size : (i + 1) * size, :] = ref[...]


def clear(cols, idx_ref, role):
    width = cols.shape[0] // 4
    y, x = idx_ref[1], idx_ref[2]

    @pl.when(role == 0)
    def _():
        cols[:, lanes(x + 2, 512)] = jnp.zeros((4 * width, 512), BF16)

    @pl.when(role == 1)
    def _():
        cols[places(lax.rem(y + 2, 4), width), :] = jnp.zeros((width, cols.shape[1]), BF16)


def mine_kernel(idx_ref, q_ref, up_ref, down_ref, near, far, cols, a_keep, a_give, b_keep, b_give, give):
    width = cols.shape[0] // 4
    for ref, first, k_ref, g_ref in ((down_ref, 0, a_keep, a_give), (up_ref, 4, b_keep, b_give)):
        for i in range(2):
            at = (first + 2 * i) * width
            k_ref[i * width : (i + 1) * width, :] = ref[at : at + width, :]
            g_ref[i * width : (i + 1) * width, :] = ref[at + width : at + 2 * width, :]
    clear(cols, idx_ref, idx_ref[4])
    for n, (d, ref) in enumerate(((0, q_ref), (1, up_ref), (3, down_ref))):
        put(cols, ref, idx_ref, idx_ref[4], d, ORDER, 0)
        for i in range(4):
            to, at = (4 * n + i) * width, (2 * i + 1) * width
            give[to : to + width, :] = ref[at : at + width, :]
    give[12 * width : 14 * width, :] = near[...]
    give[14 * width :, :] = far[...]


def row_kernel(idx_ref, k_ref, k_other, near, far, got, out_ref, out2_ref, own_ref, buf):
    width = k_ref.shape[0]
    x, zh, c = idx_ref[2], idx_ref[3], idx_ref[4]
    before, behind = lax.rem(zh + 3 + 2 * c, 4), lax.rem(zh + 5 - 2 * c, 4)
    buf[zh, 0:width] = k_ref[...]
    buf[zh, width:] = k_other[...]
    buf[before] = near[...]
    buf[behind, 0:width] = got[width : 2 * width, :]
    buf[behind, width:] = got[0:width, :]
    buf[lax.rem(zh + 2, 4), 0:width] = far[...]
    buf[lax.rem(zh + 2, 4), width:] = got[2 * width :, :]
    out_ref[...] = buf[lax.rem(x + 5 - 2 * c, 4)]
    out2_ref[...] = buf[lax.rem(x + 2, 4), 0:width]
    own_ref[...] = buf[x]


def early_kernel(idx_ref, mine, got, row_own, near, far, r_buf, acc_mine, acc_theirs, theirs):
    width = mine.shape[0] // 4
    x, c = idx_ref[2], idx_ref[4]
    this, that = places(c, width), places(1 - c, width)
    before, behind = lanes(x + 3 + 2 * c, 512), lanes(x + 5 - 2 * c, 512)
    r_buf[this, lanes(x, 512)] = row_own[0:width, :]
    r_buf[that, lanes(x, 512)] = row_own[width:, :]
    r_buf[this, before] = near[0:width, :]
    r_buf[that, before] = near[width:, :]
    r_buf[that, behind] = got[12 * width : 13 * width, :]
    r_buf[this, behind] = got[13 * width : 14 * width, :]
    r_buf[this, lanes(x + 2, 512)] = far[...]
    r_buf[that, lanes(x + 2, 512)] = got[14 * width :, :]
    clear(theirs, idx_ref, 1 - c)
    for n, d in enumerate((0, 1, 3)):
        put(theirs, got.at[4 * n * width : 4 * (n + 1) * width], idx_ref, 1 - c, d, ORDER, 0, 1)
    acc_mine[...] = lax.dot_general(r_buf[...], mine[...], NT, preferred_element_type=F32)
    acc_theirs[...] = lax.dot_general(r_buf[...], theirs[...], NT, preferred_element_type=F32)


def moment_kernel(idx_ref, r_ref, acc_mine, acc_theirs, d_a, d_b, e_a, e_b, o_ref, tall, wide, o_buf, sem):
    width = wide.shape[0]
    zl, y, x, c = idx_ref[0], idx_ref[1], idx_ref[2], idx_ref[4]
    unit = 1.0 / r_ref.shape[1]
    copies = []
    for n, (acc, role, a, b) in enumerate(((acc_mine, c, d_a, d_b), (acc_theirs, 1 - c, e_a, e_b))):
        shards = [ref[i * width : (i + 1) * width, :] for ref in (a, b) for i in range(2)]

        @pl.when(role == 0)
        def _():
            for off, v in zip(ORDER, shards):
                tall[places(lax.rem(y + off, 4), width), :] = v
            more = lax.dot_general(r_ref[:, lanes(x + 2, 512)], tall[...], NT, preferred_element_type=F32)
            o_buf[n, :, 0, :] = (acc[...] + more) * unit

        @pl.when(role == 1)
        def _():
            for off, v in zip(ORDER, shards):
                wide[:, lanes(x + off, 512)] = v
            more = lax.dot_general(r_ref[...], wide[...], NT, preferred_element_type=F32)
            o_buf[n, :, 0, :] = acc[...] * unit
            for k in range(4):

                @pl.when(lax.rem(y + 2, 4) == k)
                def _():
                    o_buf[n, :, 0, k * width : (k + 1) * width] = more * unit

        at = places(zl + role * (1 - 2 * zl), 4 * width)
        copies.append(pltpu.make_async_copy(o_buf.at[n], o_ref.at[:, :, at], sem.at[n]))
        copies[n].start()
    for cp in copies:
        cp.wait()


SMEM = pl.BlockSpec(memory_space=pltpu.SMEM)
VMEM = pl.BlockSpec(memory_space=pltpu.VMEM)
HBM = pl.BlockSpec(memory_space=pltpu.HBM)
MIB = 1024 * 1024


def shards(hidden, gain, gate_weight, up_weight):
    zl, y, x, zh, c = (lax.axis_index(a).astype(jnp.int32) for a in ("zl", "y", "x", "zh", "c"))
    features = hidden.shape[1]
    width = gate_weight.shape[1]
    rows = 2 * width
    gw, uw = gate_weight.T, up_weight.T
    g2 = gain[None, :]
    flops = 2 * 512 * features * rows
    def call(kernel, in_specs, out_shape, out_specs, scratch, limit, cost, *ins):
        return pl.pallas_call(
            kernel,
            in_specs=in_specs,
            out_specs=out_specs,
            out_shape=out_shape,
            scratch_shapes=scratch,
            compiler_params=pltpu.CompilerParams(vmem_limit_bytes=limit),
            cost_estimate=pl.CostEstimate(flops=cost, bytes_accessed=2 * MIB, transcendentals=0),
        )(*ins)

    def at(*ds):
        return jnp.stack([lax.rem(x + d, 4) for d in ds])

    send_shape = jax.ShapeDtypeStruct((rows + PAD, 512), BF16)

    def h_scratch(n):
        return [pltpu.VMEM((n, 512, features), BF16), pltpu.SemaphoreType.DMA((n,))]

    w, block2 = call(
        first_kernel, [SMEM, VMEM, HBM, HBM, HBM],
        (jax.ShapeDtypeStruct((rows, features), BF16), send_shape), (VMEM, VMEM),
        [pltpu.VMEM((2, width, features), BF16), pltpu.VMEM((512, features), BF16), pltpu.SemaphoreType.DMA((3,))],
        57 * MIB, flops, at(2), g2, gw, uw, hidden,
    )
    got2 = shift(block2, "x", 4, 2)
    block1, block3 = call(
        send_kernel, [SMEM, VMEM, HBM], (send_shape, send_shape), (VMEM, VMEM),
        h_scratch(2), 53 * MIB, 2 * flops, at(1, 3), w, hidden,
    )
    got1 = shift(block1, "x", 4, 1)
    got3 = shift(block3, "x", 4, -1)
    own_part = call(
        own_kernel, [SMEM, VMEM, HBM], jax.ShapeDtypeStruct((rows + 8, 512), F32), VMEM,
        h_scratch(1), 53 * MIB, flops, at(0), w, hidden,
    )
    keys = call(
        keys_kernel, [VMEM] * 4, jax.ShapeDtypeStruct((width, 512), BF16), VMEM, [], 16 * MIB, flops, own_part, got1, got2, got3
    )

    def after(v, *others):
        return lax.optimization_barrier((v,) + others)[0]

    def join(*parts):
        return jnp.concatenate(parts, axis=0)

    place = jnp.stack([zl, y, x, zh, c])

    def local(kernel, ins, shapes, scratch=(), indexed=True):
        single = not isinstance(shapes, tuple)
        return call(
            kernel, ([SMEM] if indexed else []) + [VMEM] * len(ins), shapes, VMEM if single else (VMEM,) * len(shapes),
            list(scratch), 12 * MIB, flops // 4, *(((place,) if indexed else ()) + tuple(ins)),
        )

    def block(n):
        return jax.ShapeDtypeStruct((n * width, 512), BF16)

    def cross(v, d, swapped, flip=0):
        pairs = []
        for i in range(4):
            for j in range(4):
                for e in range(2):
                    ni, nj = ((i + d) % 4, j) if (e == 0) != swapped else (i, (j + d) % 4)
                    pairs.append(((i * 4 + j) * 2 + e, (ni * 4 + nj) * 2 + (e ^ flip)))
        return lax.ppermute(v, ("y", "x", "c"), pairs)

    def apart(v, axis):
        return lax.ppermute(v, (axis, "c"), [(i * 2 + e, (i + 1 - 2 * e) % 4 * 2 + e) for i in range(4) for e in range(2)])

    def swap(v):
        return shift(v, "c", 2, 1)

    cols = jax.ShapeDtypeStruct((4 * width, 2048), BF16)
    partner = shift(keys, "zl", 2, 1)
    other = swap(keys)
    base = local(base_kernel, (keys, other, partner, swap(partner)), block(2))
    near = apart(join(keys, other), "zh")
    p1, p3, p2 = cross(base, -1, False), cross(base, 1, False), cross(base, 2, False)
    far = apart(near[0:width], "zh")
    q = local(pack_kernel, (base, p1, p3, after(p2, near)), block(8), indexed=False)
    q1, q3 = cross(q, -1, True), cross(q, 1, True)
    row_out, row_out2, row_own = local(
        row_kernel, (keys, other, near, far, swap(join(near, far))), (block(2), block(1), block(2)),
        [pltpu.VMEM((4, rows, 512), BF16)],
    )
    row_near, row_far = apart(row_out, "x"), shift(row_out2, "x", 4, 2)
    mine, a_keep, a_give, b_keep, b_give, give = local(
        mine_kernel, (q, q1, q3, row_near, row_far), (cols,) + (block(2),) * 4 + (block(15),)
    )
    d_a, d_b = cross(a_keep, 1, True), cross(b_keep, -1, True)
    e_a, e_b = cross(a_give, 1, True, 1), cross(b_give, -1, True, 1)
    got = swap(give)
    sums = jax.ShapeDtypeStruct((rows, 4 * width), F32)
    row_keys, acc_mine, acc_theirs = local(
        early_kernel, (mine, got, row_own, row_near, row_far),
        (jax.ShapeDtypeStruct((rows, 2048), BF16), sums, sums), [pltpu.VMEM((4 * width, 2048), BF16)],
    )
    ins = (row_keys, acc_mine, acc_theirs, d_a, d_b, e_a, e_b)
    return call(
        moment_kernel, [SMEM] + [VMEM] * len(ins), jax.ShapeDtypeStruct((rows, 1, 8 * width), F32), HBM,
        [
            pltpu.VMEM((4 * width, 512), BF16),
            pltpu.VMEM((width, 2048), BF16),
            pltpu.VMEM((2, rows, 1, 4 * width), F32),
            pltpu.SemaphoreType.DMA((2,)),
        ],
        16 * MIB, flops, place, *ins,
    )


def solution(mesh):
    fine = Mesh(mesh.devices.reshape(2, 4, 4, 4, 2), ("zl", "y", "x", "zh", "c"))
    cols = ("zl", "y", "zh", "c")
    in_specs = (P(None, "x"), P("x"), P("x", cols), P("x", cols))
    out_specs = P(("zl", "y", "x"), ("zh", "c"), None)
    return jax.shard_map(shards, mesh=fine, in_specs=in_specs, out_specs=out_specs, check_vma=False)
```

```python
import jax
import jax.numpy as jnp
from jax import lax
from jax.experimental import pallas as pl
from jax.experimental.pallas import tpu as pltpu
from jax.sharding import Mesh, PartitionSpec as P

D = 8192
EPS = 1e-05
TINY = 1e-30
F32 = jnp.float32
BF16 = jnp.bfloat16
NT = (((1,), (1,)), ((), ()))
PAD = 16


def shift(value, axis, n, by):
    return lax.ppermute(value, axis, [(i, (i + by) % n) for i in range(n)])


def encode(v):
    s = v * v
    s = s * s
    return jnp.where(v < 0, -s, s).astype(BF16)


def decode(y):
    y = y.astype(F32)
    q = lax.rsqrt(jnp.maximum(jnp.abs(y), TINY))
    return (y * q) * (q * lax.rsqrt(q))


def sumsq_row(h):
    v = h.astype(F32)
    v = v * v
    lanes = v[:, 0:128]
    for i in range(1, v.shape[1] // 128):
        lanes = lanes + v[:, i * 128 : (i + 1) * 128]
    return jnp.sum(lanes.T, axis=0, keepdims=True)


def emit_send(part, squares, o_ref, at_token):
    rows = part.shape[0]
    r = lax.rsqrt(squares + TINY)
    tokens = slice(at_token, at_token + part.shape[1])
    o_ref[0:rows, tokens] = encode(part * r)
    hi = squares.astype(BF16).astype(F32)
    rest = squares - hi
    mid = rest.astype(BF16).astype(F32)
    lo = rest - mid
    at = lax.broadcasted_iota(jnp.int32, (PAD, squares.shape[1]), 0)
    tile = jnp.where(at == 0, hi, jnp.where(at == 1, mid, jnp.where(at == 2, lo, 0.0)))
    o_ref[rows : rows + PAD, tokens] = tile.astype(BF16)


def first_kernel(idx_ref, gain_ref, gw_ref, uw_ref, h_ref, w_ref, o_ref, gu_buf, h_buf, sem):
    width = gw_ref.shape[0]
    at = pl.ds(pl.multiple_of(idx_ref[0] * 512, 512), 512)
    loads = [
        pltpu.make_async_copy(gw_ref, gu_buf.at[0], sem.at[0]),
        pltpu.make_async_copy(uw_ref, gu_buf.at[1], sem.at[1]),
        pltpu.make_async_copy(h_ref.at[at, :], h_buf, sem.at[2]),
    ]
    for cp in loads:
        cp.start()
    loads[0].wait()
    loads[1].wait()
    g = gain_ref[...]
    for i in range(2):
        w_ref[i * width : (i + 1) * width, :] = (gu_buf[i].astype(F32) * g).astype(BF16)
    loads[2].wait()
    part = lax.dot_general(w_ref[...], h_buf[...], NT, preferred_element_type=F32)
    emit_send(part, sumsq_row(h_buf[...]), o_ref, 0)


def fetch(idx_ref, h_ref, h_buf, sem):
    copies = []
    for j in range(h_buf.shape[0]):
        at = pl.ds(pl.multiple_of(idx_ref[j] * 512, 512), 512)
        copies.append(pltpu.make_async_copy(h_ref.at[at, :], h_buf.at[j], sem.at[j]))
    for cp in copies:
        cp.start()
    for cp in copies:
        cp.wait()


def send_kernel(idx_ref, w_ref, h_ref, o_ref, p_ref, h_buf, sem):
    fetch(idx_ref, h_ref, h_buf, sem)
    for k, ref in enumerate((o_ref, p_ref)):
        part = lax.dot_general(w_ref[...], h_buf[k], NT, preferred_element_type=F32)
        emit_send(part, sumsq_row(h_buf[k]), ref, 0)


def own_kernel(idx_ref, w_ref, h_ref, o_ref, h_buf, sem):
    rows = w_ref.shape[0]
    fetch(idx_ref, h_ref, h_buf, sem)
    o_ref[0:rows, :] = lax.dot_general(w_ref[...], h_buf[0], NT, preferred_element_type=F32)
    o_ref[rows : rows + 8, :] = jnp.broadcast_to(sumsq_row(h_buf[0]), (8, o_ref.shape[1]))


def keys_kernel(own_ref, p_ref, q_ref, r_ref, k_ref):
    rows = own_ref.shape[0] - 8
    width = rows // 2
    total = own_ref[rows : rows + 1, :]
    norms = []
    for ref in (p_ref, q_ref, r_ref):
        s = ref[rows : rows + PAD, :].astype(F32)
        s = s[0:1, :] + (s[1:2, :] + s[2:3, :])
        norms.append(jnp.sqrt(s + TINY))
        total = total + s
    scale = lax.rsqrt(total / D + EPS)
    mixed = own_ref[0:rows, :]
    for ref, norm in zip((p_ref, q_ref, r_ref), norms):
        mixed = mixed + decode(ref[0:rows, :]) * norm
    mixed = mixed * scale
    gate, up = mixed[0:width, :], mixed[width:rows, :]
    k_ref[...] = (gate / (1.0 + jnp.exp(-gate)) * up).astype(BF16)


ORDER = (0, 1, 3, 2)


def lanes(s, tokens):
    return pl.ds(pl.multiple_of(lax.rem(s, 4) * tokens, tokens), tokens)


def places(t, width):
    return pl.ds(pl.multiple_of(t * width, width), width)


def put(cols, ref, idx_ref, role, d, offsets, which, step=2):
    width = cols.shape[0] // 4
    y, x = idx_ref[1], idx_ref[2]
    for i, off in enumerate(offsets):
        row, lane = y + off + role * (d - off), x + d + role * (off - d)
        at = (step * i + which) * width
        cols[places(lax.rem(row, 4), width), lanes(lane, 512)] = ref[at : at + width, :]


def base_kernel(idx_ref, k_ref, k_other, p_ref, p_other, b_ref):
    width = k_ref.shape[0]
    for core, (first, second) in enumerate(((k_ref, k_other), (p_ref, p_other))):

        @pl.when(idx_ref[4] == core)
        def _():
            b_ref[0:width, :] = first[...]
            b_ref[width:, :] = second[...]


def pack_kernel(base, p1_ref, p3_ref, p2_ref, q_ref, keep, give):
    size = p1_ref.shape[0]
    for i, ref in enumerate((base, p1_ref, p3_ref, p2_ref)):
        q_ref[i * size : (i + 1) * size, :] = ref[...]
    keep[...] = p2_ref[0 : size // 2, :]
    give[...] = p2_ref[size // 2 :, :]


def clear(cols, idx_ref, role):
    width = cols.shape[0] // 4
    y, x = idx_ref[1], idx_ref[2]

    @pl.when(role == 0)
    def _():
        cols[:, lanes(x + 2, 512)] = jnp.zeros((4 * width, 512), BF16)

    @pl.when(role == 1)
    def _():
        cols[places(lax.rem(y + 2, 4), width), :] = jnp.zeros((width, cols.shape[1]), BF16)


REST = ORDER[1:]


def mine_kernel(idx_ref, q_ref, up_ref, down_ref, near, far, cols, a_keep, a_give, b_keep, b_give, give):
    width = cols.shape[0] // 4

    def shard(ref, i):
        return ref[i * width : (i + 1) * width, :]

    a_keep[0:width, :] = shard(down_ref, 2)
    a_keep[width:, :] = shard(down_ref, 6)
    a_give[...] = shard(down_ref, 3)
    b_keep[...] = shard(up_ref, 4)
    b_give[0:width, :] = shard(up_ref, 5)
    b_give[width:, :] = shard(up_ref, 7)
    clear(cols, idx_ref, idx_ref[4])
    to = 0
    for d, ref in ((0, q_ref), (1, up_ref), (3, down_ref)):
        put(cols, ref, idx_ref, idx_ref[4], d, ORDER, 0)
        for i in range(4):
            give[to : to + width, :] = shard(ref, 2 * i + 1)
            to += width
    give[to : to + 2 * width, :] = near[...]
    give[to + 2 * width :, :] = far[...]


def row_kernel(idx_ref, k_ref, k_other, near, far, got, out_ref, out2_ref, own_ref, buf):
    width = k_ref.shape[0]
    x, zh, c = idx_ref[2], idx_ref[3], idx_ref[4]
    before, behind = lax.rem(zh + 3 + 2 * c, 4), lax.rem(zh + 5 - 2 * c, 4)
    buf[zh, 0:width] = k_ref[...]
    buf[zh, width:] = k_other[...]
    buf[before] = near[...]
    buf[behind, 0:width] = got[width : 2 * width, :]
    buf[behind, width:] = got[0:width, :]
    buf[lax.rem(zh + 2, 4), 0:width] = far[...]
    buf[lax.rem(zh + 2, 4), width:] = got[2 * width :, :]
    out_ref[...] = buf[lax.rem(x + 5 - 2 * c, 4)]
    out2_ref[...] = buf[lax.rem(x + 2, 4), 0:width]
    own_ref[...] = buf[x]


def early_kernel(idx_ref, mine_in, got, z_keep, z_give, row_own, near, far, r_buf, acc_mine, acc_theirs, mine, theirs):
    width = mine.shape[0] // 4
    x, c = idx_ref[2], idx_ref[4]
    this, that = places(c, width), places(1 - c, width)
    before, behind = lanes(x + 3 + 2 * c, 512), lanes(x + 5 - 2 * c, 512)
    r_buf[this, lanes(x, 512)] = row_own[0:width, :]
    r_buf[that, lanes(x, 512)] = row_own[width:, :]
    r_buf[this, before] = near[0:width, :]
    r_buf[that, before] = near[width:, :]
    r_buf[that, behind] = got[12 * width : 13 * width, :]
    r_buf[this, behind] = got[13 * width : 14 * width, :]
    r_buf[this, lanes(x + 2, 512)] = far[...]
    r_buf[that, lanes(x + 2, 512)] = got[14 * width :, :]
    clear(theirs, idx_ref, 1 - c)
    for n, d in enumerate((0, 1, 3)):
        put(theirs, got.at[4 * n * width : 4 * (n + 1) * width], idx_ref, 1 - c, d, ORDER, 0, 1)
    put(theirs, z_keep, idx_ref, 1 - c, 2, (0,), 0, 1)
    put(mine, z_give, idx_ref, c, 2, (0,), 0, 1)
    acc_mine[...] = lax.dot_general(r_buf[...], mine[...], NT, preferred_element_type=F32)
    acc_theirs[...] = lax.dot_general(r_buf[...], theirs[...], NT, preferred_element_type=F32)


def moment_kernel(idx_ref, r_ref, acc_mine, acc_theirs, d_a, d_b, e_a, e_b, o_ref, tall, wide, o_buf, sem):
    width = wide.shape[0]
    zl, y, x, c = idx_ref[0], idx_ref[1], idx_ref[2], idx_ref[4]
    unit = 1.0 / r_ref.shape[1]
    copies = []
    where = (((0, 0), (1, 0), (0, 1)), ((0, 0), (1, 0), (1, 1)))
    for n, (acc, role, a, b) in enumerate(((acc_mine, c, d_a, d_b), (acc_theirs, 1 - c, e_a, e_b))):
        shards = [(a, b)[ref][i * width : (i + 1) * width, :] for ref, i in where[n]]

        @pl.when(role == 0)
        def _():
            tall[places(y, width), :] = jnp.zeros((width, 512), BF16)
            for off, v in zip(REST, shards):
                tall[places(lax.rem(y + off, 4), width), :] = v
            more = lax.dot_general(r_ref[:, lanes(x + 2, 512)], tall[...], NT, preferred_element_type=F32)
            o_buf[n, :, 0, :] = (acc[...] + more) * unit

        @pl.when(role == 1)
        def _():
            wide[:, lanes(x, 512)] = jnp.zeros((width, 512), BF16)
            for off, v in zip(REST, shards):
                wide[:, lanes(x + off, 512)] = v
            more = lax.dot_general(r_ref[...], wide[...], NT, preferred_element_type=F32)
            o_buf[n, :, 0, :] = acc[...] * unit
            for k in range(4):

                @pl.when(lax.rem(y + 2, 4) == k)
                def _():
                    part = slice(k * width, (k + 1) * width)
                    o_buf[n, :, 0, part] = (acc[:, part] + more) * unit

        at = places(zl + role * (1 - 2 * zl), 4 * width)
        copies.append(pltpu.make_async_copy(o_buf.at[n], o_ref.at[:, :, at], sem.at[n]))
        copies[n].start()
    for cp in copies:
        cp.wait()


SMEM = pl.BlockSpec(memory_space=pltpu.SMEM)
VMEM = pl.BlockSpec(memory_space=pltpu.VMEM)
HBM = pl.BlockSpec(memory_space=pltpu.HBM)
MIB = 1024 * 1024


def shards(hidden, gain, gate_weight, up_weight):
    zl, y, x, zh, c = (lax.axis_index(a).astype(jnp.int32) for a in ("zl", "y", "x", "zh", "c"))
    features = hidden.shape[1]
    width = gate_weight.shape[1]
    rows = 2 * width
    gw, uw = gate_weight.T, up_weight.T
    g2 = gain[None, :]
    flops = 2 * 512 * features * rows
    def call(kernel, in_specs, out_shape, out_specs, scratch, limit, cost, *ins):
        return pl.pallas_call(
            kernel,
            in_specs=in_specs,
            out_specs=out_specs,
            out_shape=out_shape,
            scratch_shapes=scratch,
            compiler_params=pltpu.CompilerParams(vmem_limit_bytes=limit),
            cost_estimate=pl.CostEstimate(flops=cost, bytes_accessed=2 * MIB, transcendentals=0),
        )(*ins)

    def at(*ds):
        return jnp.stack([lax.rem(x + d, 4) for d in ds])

    send_shape = jax.ShapeDtypeStruct((rows + PAD, 512), BF16)

    def h_scratch(n):
        return [pltpu.VMEM((n, 512, features), BF16), pltpu.SemaphoreType.DMA((n,))]

    w, block2 = call(
        first_kernel, [SMEM, VMEM, HBM, HBM, HBM],
        (jax.ShapeDtypeStruct((rows, features), BF16), send_shape), (VMEM, VMEM),
        [pltpu.VMEM((2, width, features), BF16), pltpu.VMEM((512, features), BF16), pltpu.SemaphoreType.DMA((3,))],
        57 * MIB, flops, at(2), g2, gw, uw, hidden,
    )
    got2 = shift(block2, "x", 4, 2)
    block1, block3 = call(
        send_kernel, [SMEM, VMEM, HBM], (send_shape, send_shape), (VMEM, VMEM),
        h_scratch(2), 53 * MIB, 2 * flops, at(1, 3), w, hidden,
    )
    got1 = shift(block1, "x", 4, 1)
    got3 = shift(block3, "x", 4, -1)
    own_part = call(
        own_kernel, [SMEM, VMEM, HBM], jax.ShapeDtypeStruct((rows + 8, 512), F32), VMEM,
        h_scratch(1), 53 * MIB, flops, at(0), w, hidden,
    )
    keys = call(
        keys_kernel, [VMEM] * 4, jax.ShapeDtypeStruct((width, 512), BF16), VMEM, [], 16 * MIB, flops, own_part, got1, got2, got3
    )

    def after(v, *others):
        return lax.optimization_barrier((v,) + others)[0]

    def join(*parts):
        return jnp.concatenate(parts, axis=0)

    place = jnp.stack([zl, y, x, zh, c])

    def local(kernel, ins, shapes, scratch=(), indexed=True):
        single = not isinstance(shapes, tuple)
        return call(
            kernel, ([SMEM] if indexed else []) + [VMEM] * len(ins), shapes, VMEM if single else (VMEM,) * len(shapes),
            list(scratch), 12 * MIB, flops // 4, *(((place,) if indexed else ()) + tuple(ins)),
        )

    def block(n):
        return jax.ShapeDtypeStruct((n * width, 512), BF16)

    def cross(v, d, swapped, flip=0):
        pairs = []
        for i in range(4):
            for j in range(4):
                for e in range(2):
                    ni, nj = ((i + d) % 4, j) if (e == 0) != swapped else (i, (j + d) % 4)
                    pairs.append(((i * 4 + j) * 2 + e, (ni * 4 + nj) * 2 + (e ^ flip)))
        return lax.ppermute(v, ("y", "x", "c"), pairs)

    def apart(v, axis):
        return lax.ppermute(v, (axis, "c"), [(i * 2 + e, (i + 1 - 2 * e) % 4 * 2 + e) for i in range(4) for e in range(2)])

    def swap(v):
        return shift(v, "c", 2, 1)

    cols = jax.ShapeDtypeStruct((4 * width, 2048), BF16)
    partner = shift(keys, "zl", 2, 1)
    other = swap(keys)
    base = local(base_kernel, (keys, other, partner, swap(partner)), block(2))
    near = apart(after(join(keys, other), base), "zh")
    p1, p3, p2 = cross(base, -1, False), cross(base, 1, False), cross(base, 2, False)
    far = apart(near[0:width], "zh")
    q, z_keep, z_give = local(pack_kernel, (base, p1, p3, p2), (block(8), block(1), block(1)), indexed=False)
    z_keep = shift(z_keep, "zl", 2, 1)
    z_give = lax.ppermute(z_give, ("zl", "c"), [(0, 3), (1, 2), (2, 1), (3, 0)])
    q1, q3 = cross(q, -1, True), cross(q, 1, True)
    row_out, row_out2, row_own = local(
        row_kernel, (keys, other, near, far, swap(join(near, far))), (block(2), block(1), block(2)),
        [pltpu.VMEM((4, rows, 512), BF16)],
    )
    row_near, row_far = apart(row_out, "x"), shift(row_out2, "x", 4, 2)
    mine, a_keep, a_give, b_keep, b_give, give = local(
        mine_kernel, (q, q1, after(q3, z_keep, z_give), row_near, row_far),
        (cols, block(2), block(1), block(1), block(2), block(15)),
    )
    d_a, d_b = cross(a_keep, 1, True), cross(b_keep, -1, True)
    e_a, e_b = cross(a_give, 1, True, 1), cross(b_give, -1, True, 1)
    got = swap(give)
    sums = jax.ShapeDtypeStruct((rows, 4 * width), F32)
    row_keys, acc_mine, acc_theirs, _ = pl.pallas_call(
        early_kernel,
        in_specs=[SMEM] + [VMEM] * 7,
        out_specs=(VMEM,) * 4,
        out_shape=(jax.ShapeDtypeStruct((rows, 2048), BF16), sums, sums, cols),
        scratch_shapes=[pltpu.VMEM((4 * width, 2048), BF16)],
        input_output_aliases={1: 3},
        compiler_params=pltpu.CompilerParams(vmem_limit_bytes=12 * MIB),
        cost_estimate=pl.CostEstimate(flops=flops // 4, bytes_accessed=2 * MIB, transcendentals=0),
    )(place, mine, got, z_keep, z_give, row_own, row_near, row_far)
    ins = (row_keys, acc_mine, acc_theirs, d_a, d_b, e_a, e_b)
    return call(
        moment_kernel, [SMEM] + [VMEM] * len(ins), jax.ShapeDtypeStruct((rows, 1, 8 * width), F32), HBM,
        [
            pltpu.VMEM((4 * width, 512), BF16),
            pltpu.VMEM((width, 2048), BF16),
            pltpu.VMEM((2, rows, 1, 4 * width), F32),
            pltpu.SemaphoreType.DMA((2,)),
        ],
        16 * MIB, flops, place, *ins,
    )


def solution(mesh):
    fine = Mesh(mesh.devices.reshape(2, 4, 4, 4, 2), ("zl", "y", "x", "zh", "c"))
    cols = ("zl", "y", "zh", "c")
    in_specs = (P(None, "x"), P("x"), P("x", cols), P("x", cols))
    out_specs = P(("zl", "y", "x"), ("zh", "c"), None)
    return jax.shard_map(shards, mesh=fine, in_specs=in_specs, out_specs=out_specs, check_vma=False)
```

```python
import jax
import jax.numpy as jnp
from jax import lax
from jax.experimental import pallas as pl
from jax.experimental.pallas import tpu as pltpu
from jax.sharding import Mesh, PartitionSpec as P

D = 8192
EPS = 1e-05
TINY = 1e-30
F32 = jnp.float32
BF16 = jnp.bfloat16
NT = (((1,), (1,)), ((), ()))
PAD = 16


def shift(value, axis, n, by):
    return lax.ppermute(value, axis, [(i, (i + by) % n) for i in range(n)])


def encode(v):
    s = v * v
    s = s * s
    return jnp.where(v < 0, -s, s).astype(BF16)


def decode(y):
    y = y.astype(F32)
    q = lax.rsqrt(jnp.maximum(jnp.abs(y), TINY))
    return (y * q) * (q * lax.rsqrt(q))


def sumsq_row(h):
    v = h.astype(F32)
    v = v * v
    lanes = v[:, 0:128]
    for i in range(1, v.shape[1] // 128):
        lanes = lanes + v[:, i * 128 : (i + 1) * 128]
    return jnp.sum(lanes.T, axis=0, keepdims=True)


def emit_send(part, squares, o_ref, at_token):
    rows = part.shape[0]
    r = lax.rsqrt(squares + TINY)
    tokens = slice(at_token, at_token + part.shape[1])
    o_ref[0:rows, tokens] = encode(part * r)
    hi = squares.astype(BF16).astype(F32)
    rest = squares - hi
    mid = rest.astype(BF16).astype(F32)
    lo = rest - mid
    at = lax.broadcasted_iota(jnp.int32, (PAD, squares.shape[1]), 0)
    tile = jnp.where(at == 0, hi, jnp.where(at == 1, mid, jnp.where(at == 2, lo, 0.0)))
    o_ref[rows : rows + PAD, tokens] = tile.astype(BF16)


def first_kernel(idx_ref, gain_ref, gw_ref, uw_ref, h_ref, w_ref, o_ref, gu_buf, h_buf, sem):
    width = gw_ref.shape[0]
    at = pl.ds(pl.multiple_of(idx_ref[0] * 512, 512), 512)
    loads = [
        pltpu.make_async_copy(gw_ref, gu_buf.at[0], sem.at[0]),
        pltpu.make_async_copy(uw_ref, gu_buf.at[1], sem.at[1]),
        pltpu.make_async_copy(h_ref.at[at, :], h_buf, sem.at[2]),
    ]
    for cp in loads:
        cp.start()
    loads[0].wait()
    loads[1].wait()
    g = gain_ref[...]
    for i in range(2):
        w_ref[i * width : (i + 1) * width, :] = (gu_buf[i].astype(F32) * g).astype(BF16)
    loads[2].wait()
    part = lax.dot_general(w_ref[...], h_buf[...], NT, preferred_element_type=F32)
    emit_send(part, sumsq_row(h_buf[...]), o_ref, 0)


def fetch(idx_ref, h_ref, h_buf, sem):
    copies = []
    for j in range(h_buf.shape[0]):
        at = pl.ds(pl.multiple_of(idx_ref[j] * 512, 512), 512)
        copies.append(pltpu.make_async_copy(h_ref.at[at, :], h_buf.at[j], sem.at[j]))
    for cp in copies:
        cp.start()
    for cp in copies:
        cp.wait()


def send_kernel(idx_ref, w_ref, h_ref, o_ref, p_ref, h_buf, sem):
    fetch(idx_ref, h_ref, h_buf, sem)
    for k, ref in enumerate((o_ref, p_ref)):
        part = lax.dot_general(w_ref[...], h_buf[k], NT, preferred_element_type=F32)
        emit_send(part, sumsq_row(h_buf[k]), ref, 0)


def own_kernel(idx_ref, w_ref, h_ref, o_ref, h_buf, sem):
    rows = w_ref.shape[0]
    fetch(idx_ref, h_ref, h_buf, sem)
    o_ref[0:rows, :] = lax.dot_general(w_ref[...], h_buf[0], NT, preferred_element_type=F32)
    o_ref[rows : rows + 8, :] = jnp.broadcast_to(sumsq_row(h_buf[0]), (8, o_ref.shape[1]))


def keys_kernel(own_ref, p_ref, q_ref, r_ref, k_ref):
    rows = own_ref.shape[0] - 8
    width = rows // 2
    total = own_ref[rows : rows + 1, :]
    norms = []
    for ref in (p_ref, q_ref, r_ref):
        s = ref[rows : rows + PAD, :].astype(F32)
        s = s[0:1, :] + (s[1:2, :] + s[2:3, :])
        norms.append(jnp.sqrt(s + TINY))
        total = total + s
    scale = lax.rsqrt(total / D + EPS)
    mixed = own_ref[0:rows, :]
    for ref, norm in zip((p_ref, q_ref, r_ref), norms):
        mixed = mixed + decode(ref[0:rows, :]) * norm
    mixed = mixed * scale
    gate, up = mixed[0:width, :], mixed[width:rows, :]
    k_ref[...] = (gate / (1.0 + jnp.exp(-gate)) * up).astype(BF16)


ORDER = (0, 1, 3, 2)


def lanes(s, tokens):
    return pl.ds(pl.multiple_of(lax.rem(s, 4) * tokens, tokens), tokens)


def places(t, width):
    return pl.ds(pl.multiple_of(t * width, width), width)


def put(cols, ref, idx_ref, role, d, offsets, which, step=2):
    width = cols.shape[0] // 4
    y, x = idx_ref[1], idx_ref[2]
    for i, off in enumerate(offsets):
        row, lane = y + off + role * (d - off), x + d + role * (off - d)
        at = (step * i + which) * width
        cols[places(lax.rem(row, 4), width), lanes(lane, 512)] = ref[at : at + width, :]


def base_kernel(idx_ref, k_ref, k_other, p_ref, p_other, b_ref):
    width = k_ref.shape[0]
    for core, (first, second) in enumerate(((k_ref, k_other), (p_ref, p_other))):

        @pl.when(idx_ref[4] == core)
        def _():
            b_ref[0:width, :] = first[...]
            b_ref[width:, :] = second[...]


def pack_kernel(*refs):
    size = refs[0].shape[0]
    for i, ref in enumerate(refs[:4]):
        refs[4][i * size : (i + 1) * size, :] = ref[...]


def clear(cols, idx_ref, role):
    width = cols.shape[0] // 4
    y, x = idx_ref[1], idx_ref[2]

    @pl.when(role == 0)
    def _():
        cols[:, lanes(x + 2, 512)] = jnp.zeros((4 * width, 512), BF16)

    @pl.when(role == 1)
    def _():
        cols[places(lax.rem(y + 2, 4), width), :] = jnp.zeros((width, cols.shape[1]), BF16)


REST = ORDER[1:]


def mine_kernel(idx_ref, q_ref, up_ref, down_ref, near, far, z_ref, cols, a_keep, a_give, b_keep, b_give, give):
    width = cols.shape[0] // 4

    def shard(ref, i):
        return ref[i * width : (i + 1) * width, :]

    a_keep[0:width, :] = shard(down_ref, 2)
    a_keep[width:, :] = shard(down_ref, 6)
    a_give[...] = shard(down_ref, 3)
    b_keep[...] = shard(up_ref, 4)
    b_give[0:width, :] = shard(up_ref, 5)
    b_give[width:, :] = shard(up_ref, 7)
    clear(cols, idx_ref, idx_ref[4])
    to = 0
    for d, ref in ((0, q_ref), (1, up_ref), (3, down_ref)):
        put(cols, ref, idx_ref, idx_ref[4], d, ORDER, 0)
        for i in range(4):
            give[to : to + width, :] = shard(ref, 2 * i + 1)
            to += width
    put(cols, z_ref, idx_ref, idx_ref[4], 2, (0,), 1)
    give[to : to + width, :] = shard(z_ref, 0)
    give[to + width : to + 3 * width, :] = near[...]
    give[to + 3 * width :, :] = far[...]


def row_kernel(idx_ref, k_ref, k_other, near, far, got, out_ref, out2_ref, own_ref, buf):
    width = k_ref.shape[0]
    x, zh, c = idx_ref[2], idx_ref[3], idx_ref[4]
    before, behind = lax.rem(zh + 3 + 2 * c, 4), lax.rem(zh + 5 - 2 * c, 4)
    buf[zh, 0:width] = k_ref[...]
    buf[zh, width:] = k_other[...]
    buf[before] = near[...]
    buf[behind, 0:width] = got[width : 2 * width, :]
    buf[behind, width:] = got[0:width, :]
    buf[lax.rem(zh + 2, 4), 0:width] = far[...]
    buf[lax.rem(zh + 2, 4), width:] = got[2 * width :, :]
    out_ref[...] = buf[lax.rem(x + 5 - 2 * c, 4)]
    out2_ref[...] = buf[lax.rem(x + 2, 4), 0:width]
    own_ref[...] = buf[x]


def early_kernel(idx_ref, mine, got, row_own, near, far, r_buf, acc_mine, acc_theirs, theirs):
    width = mine.shape[0] // 4
    x, c = idx_ref[2], idx_ref[4]
    this, that = places(c, width), places(1 - c, width)
    before, behind = lanes(x + 3 + 2 * c, 512), lanes(x + 5 - 2 * c, 512)
    r_buf[this, lanes(x, 512)] = row_own[0:width, :]
    r_buf[that, lanes(x, 512)] = row_own[width:, :]
    r_buf[this, before] = near[0:width, :]
    r_buf[that, before] = near[width:, :]
    r_buf[that, behind] = got[13 * width : 14 * width, :]
    r_buf[this, behind] = got[14 * width : 15 * width, :]
    r_buf[this, lanes(x + 2, 512)] = far[...]
    r_buf[that, lanes(x + 2, 512)] = got[15 * width :, :]
    clear(theirs, idx_ref, 1 - c)
    for n, d in enumerate((0, 1, 3)):
        put(theirs, got.at[4 * n * width : 4 * (n + 1) * width], idx_ref, 1 - c, d, ORDER, 0, 1)
    put(theirs, got.at[12 * width : 13 * width], idx_ref, 1 - c, 2, (0,), 0, 1)
    acc_mine[...] = lax.dot_general(r_buf[...], mine[...], NT, preferred_element_type=F32)
    acc_theirs[...] = lax.dot_general(r_buf[...], theirs[...], NT, preferred_element_type=F32)


def moment_kernel(idx_ref, r_ref, acc_mine, acc_theirs, d_a, d_b, e_a, e_b, o_ref, tall, wide, o_buf, sem):
    width = wide.shape[0]
    zl, y, x, c = idx_ref[0], idx_ref[1], idx_ref[2], idx_ref[4]
    unit = 1.0 / r_ref.shape[1]
    copies = []
    where = (((0, 0), (1, 0), (0, 1)), ((0, 0), (1, 0), (1, 1)))
    for n, (acc, role, a, b) in enumerate(((acc_mine, c, d_a, d_b), (acc_theirs, 1 - c, e_a, e_b))):
        shards = [(a, b)[ref][i * width : (i + 1) * width, :] for ref, i in where[n]]

        @pl.when(role == 0)
        def _():
            tall[places(y, width), :] = jnp.zeros((width, 512), BF16)
            for off, v in zip(REST, shards):
                tall[places(lax.rem(y + off, 4), width), :] = v
            more = lax.dot_general(r_ref[:, lanes(x + 2, 512)], tall[...], NT, preferred_element_type=F32)
            o_buf[n, :, 0, :] = (acc[...] + more) * unit

        @pl.when(role == 1)
        def _():
            wide[:, lanes(x, 512)] = jnp.zeros((width, 512), BF16)
            for off, v in zip(REST, shards):
                wide[:, lanes(x + off, 512)] = v
            more = lax.dot_general(r_ref[...], wide[...], NT, preferred_element_type=F32)
            o_buf[n, :, 0, :] = acc[...] * unit
            for k in range(4):

                @pl.when(lax.rem(y + 2, 4) == k)
                def _():
                    part = slice(k * width, (k + 1) * width)
                    o_buf[n, :, 0, part] = (acc[:, part] + more) * unit

        at = places(zl + role * (1 - 2 * zl), 4 * width)
        copies.append(pltpu.make_async_copy(o_buf.at[n], o_ref.at[:, :, at], sem.at[n]))
        copies[n].start()
    for cp in copies:
        cp.wait()


SMEM = pl.BlockSpec(memory_space=pltpu.SMEM)
VMEM = pl.BlockSpec(memory_space=pltpu.VMEM)
HBM = pl.BlockSpec(memory_space=pltpu.HBM)
MIB = 1024 * 1024


def shards(hidden, gain, gate_weight, up_weight):
    zl, y, x, zh, c = (lax.axis_index(a).astype(jnp.int32) for a in ("zl", "y", "x", "zh", "c"))
    features = hidden.shape[1]
    width = gate_weight.shape[1]
    rows = 2 * width
    gw, uw = gate_weight.T, up_weight.T
    g2 = gain[None, :]
    flops = 2 * 512 * features * rows
    def call(kernel, in_specs, out_shape, out_specs, scratch, limit, cost, *ins):
        return pl.pallas_call(
            kernel,
            in_specs=in_specs,
            out_specs=out_specs,
            out_shape=out_shape,
            scratch_shapes=scratch,
            compiler_params=pltpu.CompilerParams(vmem_limit_bytes=limit),
            cost_estimate=pl.CostEstimate(flops=cost, bytes_accessed=2 * MIB, transcendentals=0),
        )(*ins)

    def at(*ds):
        return jnp.stack([lax.rem(x + d, 4) for d in ds])

    send_shape = jax.ShapeDtypeStruct((rows + PAD, 512), BF16)

    def h_scratch(n):
        return [pltpu.VMEM((n, 512, features), BF16), pltpu.SemaphoreType.DMA((n,))]

    w, block2 = call(
        first_kernel, [SMEM, VMEM, HBM, HBM, HBM],
        (jax.ShapeDtypeStruct((rows, features), BF16), send_shape), (VMEM, VMEM),
        [pltpu.VMEM((2, width, features), BF16), pltpu.VMEM((512, features), BF16), pltpu.SemaphoreType.DMA((3,))],
        57 * MIB, flops, at(2), g2, gw, uw, hidden,
    )
    got2 = shift(block2, "x", 4, 2)
    block1, block3 = call(
        send_kernel, [SMEM, VMEM, HBM], (send_shape, send_shape), (VMEM, VMEM),
        h_scratch(2), 53 * MIB, 2 * flops, at(1, 3), w, hidden,
    )
    got1 = shift(block1, "x", 4, 1)
    got3 = shift(block3, "x", 4, -1)
    own_part = call(
        own_kernel, [SMEM, VMEM, HBM], jax.ShapeDtypeStruct((rows + 8, 512), F32), VMEM,
        h_scratch(1), 53 * MIB, flops, at(0), w, hidden,
    )
    keys = call(
        keys_kernel, [VMEM] * 4, jax.ShapeDtypeStruct((width, 512), BF16), VMEM, [], 16 * MIB, flops, own_part, got1, got2, got3
    )

    def after(v, *others):
        return lax.optimization_barrier((v,) + others)[0]

    def join(*parts):
        return jnp.concatenate(parts, axis=0)

    place = jnp.stack([zl, y, x, zh, c])

    def local(kernel, ins, shapes, scratch=(), indexed=True):
        single = not isinstance(shapes, tuple)
        return call(
            kernel, ([SMEM] if indexed else []) + [VMEM] * len(ins), shapes, VMEM if single else (VMEM,) * len(shapes),
            list(scratch), 12 * MIB, flops // 4, *(((place,) if indexed else ()) + tuple(ins)),
        )

    def block(n):
        return jax.ShapeDtypeStruct((n * width, 512), BF16)

    def cross(v, d, swapped, flip=0):
        pairs = []
        for i in range(4):
            for j in range(4):
                for e in range(2):
                    ni, nj = ((i + d) % 4, j) if (e == 0) != swapped else (i, (j + d) % 4)
                    pairs.append(((i * 4 + j) * 2 + e, (ni * 4 + nj) * 2 + (e ^ flip)))
        return lax.ppermute(v, ("y", "x", "c"), pairs)

    def apart(v, axis):
        return lax.ppermute(v, (axis, "c"), [(i * 2 + e, (i + 1 - 2 * e) % 4 * 2 + e) for i in range(4) for e in range(2)])

    def swap(v):
        return shift(v, "c", 2, 1)

    cols = jax.ShapeDtypeStruct((4 * width, 2048), BF16)
    partner = shift(keys, "zl", 2, 1)
    other = swap(keys)
    base = local(base_kernel, (keys, other, partner, swap(partner)), block(2))
    near = apart(after(join(keys, other), base), "zh")
    p1, p3, p2 = cross(base, -1, False), cross(base, 1, False), cross(base, 2, False)
    far = apart(near[0:width], "zh")
    q = local(pack_kernel, (base, p1, p3, p2), block(8), indexed=False)
    z_pair = lax.ppermute(p2, ("zl", "c"), [(0, 3), (1, 2), (2, 1), (3, 0)])
    q1, q3 = cross(q, -1, True), cross(q, 1, True)
    row_out, row_out2, row_own = local(
        row_kernel, (keys, other, near, far, swap(join(near, far))), (block(2), block(1), block(2)),
        [pltpu.VMEM((4, rows, 512), BF16)],
    )
    row_near, row_far = apart(row_out, "x"), shift(row_out2, "x", 4, 2)
    mine, a_keep, a_give, b_keep, b_give, give = local(
        mine_kernel, (q, q1, q3, row_near, row_far, z_pair),
        (cols, block(2), block(1), block(1), block(2), block(16)),
    )
    d_a, d_b = cross(a_keep, 1, True), cross(b_keep, -1, True)
    e_a, e_b = cross(a_give, 1, True, 1), cross(b_give, -1, True, 1)
    got = swap(give)
    sums = jax.ShapeDtypeStruct((rows, 4 * width), F32)
    row_keys, acc_mine, acc_theirs = local(
        early_kernel, (mine, got, row_own, row_near, row_far),
        (jax.ShapeDtypeStruct((rows, 2048), BF16), sums, sums), [pltpu.VMEM((4 * width, 2048), BF16)],
    )
    ins = (row_keys, acc_mine, acc_theirs, d_a, d_b, e_a, e_b)
    return call(
        moment_kernel, [SMEM] + [VMEM] * len(ins), jax.ShapeDtypeStruct((rows, 1, 8 * width), F32), HBM,
        [
            pltpu.VMEM((4 * width, 512), BF16),
            pltpu.VMEM((width, 2048), BF16),
            pltpu.VMEM((2, rows, 1, 4 * width), F32),
            pltpu.SemaphoreType.DMA((2,)),
        ],
        16 * MIB, flops, place, *ins,
    )


def solution(mesh):
    fine = Mesh(mesh.devices.reshape(2, 4, 4, 4, 2), ("zl", "y", "x", "zh", "c"))
    cols = ("zl", "y", "zh", "c")
    in_specs = (P(None, "x"), P("x"), P("x", cols), P("x", cols))
    out_specs = P(("zl", "y", "x"), ("zh", "c"), None)
    return jax.shard_map(shards, mesh=fine, in_specs=in_specs, out_specs=out_specs, check_vma=False)
```
